1024 devices in a mesh: row: 128 (over y, z), col: 8 (over x, core).
Axes of the slice: x: 4, y: 4, z: 32, core: 2. Of those that a mesh axis runs over, the one named last changes fastest.
Arguments:
- right_side: float32 [128, 8, 8, 128], P('row', 'col'), may hold values from -6 to 6
- block_values: bfloat16 [128, 8, 8, 4, 128, 128], P('row', 'col'), may hold values from -0.25 to 0.25
- block_columns: int32 [128, 8, 8, 4], P('row', 'col'), may hold values from 0 to 71
- live_slots: int32 [128, 8, 8], P('row', 'col'), may hold values from 1 to 4
- row_scale: float32 [128, 8, 8, 128], P('row', 'col'), may hold values from 1 to 4
Outputs:
- solution_field: float32 [128, 8, 8, 128], P('row', 'col')
- hessenberg: float32 [5, 4], replicated
The draws below stay inside these ranges and needn't reach their ends.
Inputs may be any that keep to these rules, and one draw needn't show every extreme that they name: `block_columns`: an entry q names block q % 8 of the device at grid offset (q // 24 - 1, (q // 8) % 3 - 1); blocks outside the grid are zero. Only the first live_slots slots of a block row are used.
All inputs are finite; a program needn't handle non-finite values.
Results may differ from the reference program's by a relative error of at most 0.0012.
Values may be sent and summed in bfloat16 or wider, within the bound.
No kernel may reach another device: no remote copies, remote signals or barrier semaphores. Data moves between devices by JAX's collectives and lax.ppermute only.
A program may use at most 32 MiB of HBM per device.

```python
import math
import jax
import jax.numpy as jnp
from jax import lax

NB = 8
BS = 128
SLOTS = 4
ITERS = 4
N_ROW = 128
N_COL = 8


def place_ends(drawn, rng, low, largest):
    longest = drawn.shape.index(max(drawn.shape))
    spots = []
    for shift in (0, 1):
        where = [jax.random.randint(jax.random.fold_in(rng, axis), (), 0, length) for axis, length in enumerate(drawn.shape)]
        where[longest] = (where[longest] + shift) % drawn.shape[longest]
        spots.append(tuple(where))
    return drawn.at[spots[0]].set(low).at[spots[1]].set(largest)


def block_scale(own_key, shape, split, least, top_value):
    gain = 1.0
    for axis_at, shards_of in split:
        heights = jax.random.uniform(jax.random.fold_in(jax.random.fold_in(own_key, 6), axis_at), (shards_of,), jnp.float32, least / len(split), top_value / len(split))
        gain = gain * jnp.repeat(jnp.exp(heights), shape[axis_at] // shards_of).reshape((-1,) + (1,) * (len(shape) - 1 - axis_at))
    return gain


def normal_values(stream_key, shape, spread, bound, split=(), kind=jnp.bfloat16):
    values = spread * jax.random.normal(stream_key, shape, jnp.float32)
    if split:
        values = values * block_scale(stream_key, shape, split, -0.22, 0.18)
    return jnp.clip(values, -bound, bound).astype(kind)


def setup_inputs(seed: int = 0) -> dict:
    keys = jax.random.split(jax.random.key(seed), 6)
    right_side = normal_values(keys[0], (N_ROW, N_COL, NB, BS), 1.0, 6.0, ((0, 128), (1, 8)), jnp.float32)
    block_values = normal_values(keys[1], (N_ROW, N_COL, NB, SLOTS, BS, BS), (BS * SLOTS) ** -0.5, 0.25, ((0, 128), (1, 8)))
    block_columns = place_ends(jax.random.randint(keys[2], (N_ROW, N_COL, NB, SLOTS), 0, 9 * NB), jax.random.fold_in(keys[2], 1), 0, (9 * NB) - 1).astype(jnp.int32)
    live_slots = place_ends(jax.random.randint(keys[3], (N_ROW, N_COL, NB), 1, SLOTS + 1), jax.random.fold_in(keys[3], 1), 1, SLOTS).astype(jnp.int32)
    row_scale = jnp.clip(jnp.exp(math.log(4.0) - 1.3862944 * jax.random.uniform(keys[4], (N_ROW, N_COL, NB, BS), jnp.float32) ** block_scale(keys[4], (N_ROW, N_COL, NB, BS), ((0, 128), (1, 8)), -0.2, 0.2)), 1.0, 4.0)
    return dict(right_side=right_side, block_values=block_values, block_columns=block_columns, live_slots=live_slots, row_scale=row_scale)


def neighbour_index(block_columns):
    row_count, col_count, block_count, slot_count = block_columns.shape
    grid_rows = jnp.arange(row_count, dtype=jnp.int32)[:, None, None, None]
    grid_cols = jnp.arange(col_count, dtype=jnp.int32)[None, :, None, None]
    offset_row = block_columns // (3 * block_count)
    offset_col = block_columns // block_count % 3
    within = block_columns % block_count
    return (((grid_rows + offset_row) * (col_count + 2) + grid_cols + offset_col) * block_count + within).astype(jnp.int32)

def operate(field, block_values, flat_index, live_mask, row_scale):
    rounded = field.astype(jnp.bfloat16)
    padded = jnp.pad(rounded, ((1, 1), (1, 1), (0, 0), (0, 0)))
    flat = padded.reshape(-1, rounded.shape[-1])
    picked = flat[flat_index] * live_mask

    def one_row(pair):
        values, pieces = pair
        return jnp.einsum('cnsij,cnsj->cni', values.astype(jnp.float32), pieces.astype(jnp.float32), precision=lax.Precision.HIGHEST)
    product = lax.map(one_row, (block_values, picked))
    return row_scale * field + product

def least_squares(hessenberg, initial_norm):
    gram = jnp.dot(hessenberg.T, hessenberg, precision=lax.Precision.HIGHEST)
    target = initial_norm * hessenberg[0, :]
    factor = jnp.linalg.cholesky(gram)
    steps_count = gram.shape[0]
    forward = []
    for ordinal in range(steps_count):
        accum = target[ordinal]
        for other in range(ordinal):
            accum = accum - factor[ordinal, other] * forward[other]
        forward.append(accum / factor[ordinal, ordinal])
    backward = [None] * steps_count
    for ordinal in reversed(range(steps_count)):
        accum = forward[ordinal]
        for other in range(ordinal + 1, steps_count):
            accum = accum - factor[other, ordinal] * backward[other]
        backward[ordinal] = accum / factor[ordinal, ordinal]
    return backward

def reference(right_side, block_values, block_columns, live_slots, row_scale):
    flat_index = neighbour_index(block_columns)
    slot_count = block_columns.shape[-1]
    live_mask = (jnp.arange(slot_count, dtype=jnp.int32)[None, None, None, :] < live_slots[..., None]).astype(jnp.bfloat16)[..., None]
    first_image = operate(right_side, block_values, flat_index, live_mask, row_scale)
    self_dot = jnp.sum(right_side * right_side)
    cross_dot = jnp.sum(right_side * first_image)
    image_dot = jnp.sum(first_image * first_image)
    initial_norm = jnp.sqrt(self_dot)
    basis = [right_side / initial_norm]
    residue = first_image / initial_norm
    projections = jnp.stack([cross_dot / self_dot])
    norm_square = image_dot / self_dot
    columns = []
    for iteration in range(ITERS):
        if iteration > 0:
            residue = operate(basis[-1], block_values, flat_index, live_mask, row_scale)
            projections = jnp.stack([jnp.sum(vector * residue) for vector in basis])
            norm_square = jnp.sum(residue * residue)
        height = jnp.sqrt(norm_square - jnp.sum(projections * projections))
        columns.append(jnp.concatenate([projections, height[None], jnp.zeros((ITERS - iteration - 1,), jnp.float32)]))
        if iteration + 1 < ITERS:
            for ordinal in range(len(basis)):
                residue = residue - projections[ordinal] * basis[ordinal]
            basis.append(residue / height)
    hessenberg = jnp.stack(columns, axis=1)
    weights = least_squares(hessenberg, initial_norm)
    solution_field = weights[0] * basis[0]
    for ordinal in range(1, ITERS):
        solution_field = solution_field + weights[ordinal] * basis[ordinal]
    return (solution_field, hessenberg)
```

```python
import jax
import jax.numpy as jnp
from jax import lax
from jax.experimental import pallas as pl
from jax.experimental.pallas import tpu as pltpu
from jax.sharding import Mesh
from jax.sharding import PartitionSpec as P

ITERS = 4
NB = 8
BS = 128
SLOTS = 4
ROW = ("y", "z")
COL = ("x", "core")
PLANE = ("y", "x", "core")
SHIFT = 2.2
PAIRS = [(i, j) for j in range(ITERS + 1) for i in range(j + 1)]
F32 = jnp.float32
BF16 = jnp.bfloat16


def swaps(count):
    even = [(i, i ^ 1) for i in range(count)]
    odd = []
    for i in range(1, count - 1, 2):
        odd += [(i, i + 1), (i + 1, i)]
    return even, odd


def exchange(field, rows, cols):
    even, odd = swaps(rows)
    beside = jnp.stack(
        [field, lax.ppermute(field, ROW, even), lax.ppermute(field, ROW, odd)]
    )
    even, odd = swaps(cols)
    return (
        beside,
        lax.ppermute(beside, COL, even),
        lax.ppermute(beside, COL, odd),
    )


def fill(halo, parts):
    for at, part in enumerate(parts):
        for row in range(3):
            halo[pl.ds((at * 3 + row) * NB, NB), :] = part[row]
    halo[pl.ds(9 * NB, NB), :] = jnp.zeros((NB, BS), F32)


def multiply(index, halo, values, fine):
    sublane = lax.broadcasted_iota(jnp.int32, (NB, BS), 0)
    total = jnp.zeros((2 * NB, BS), F32)
    for n in range(NB):
        pieces = []
        for s in range(SLOTS):
            row = halo[pl.ds(index[n * SLOTS + s], 1), :]
            row = jnp.where(sublane == n, jnp.broadcast_to(row, (NB, BS)), 0.0)
            high = row.astype(BF16).astype(F32)
            low = row - high if fine else jnp.zeros_like(row)
            pieces.append(jnp.concatenate([high, low], axis=0).astype(BF16))
        left = jnp.concatenate(pieces, axis=1)
        right = jnp.concatenate([values[n * SLOTS + s] for s in range(SLOTS)], axis=1)
        total = total + lax.dot_general(
            left, right, (((1,), (1,)), ((), ())), preferred_element_type=F32
        )
    return total[:NB] + total[NB:]


def apply_kernel(fine, index, own, even, odd, values, scale, out, halo):
    fill(halo, (own, even, odd))
    field = own[0]
    product = multiply(index, halo, values, fine)
    out[...] = (scale[...] * field - SHIFT * field) + product


def last_kernel(index, own, even, odd, values, scale, u0, u1, u2, out, halo):
    fill(halo, (own, even, odd))
    field = own[0]
    product = multiply(index, halo, values, True)
    u4 = (scale[...] * field - SHIFT * field) + product
    fields = (u0[...], u1[...], u2[...], field, u4)
    lane = lax.broadcasted_iota(jnp.int32, (1, BS), 1)
    dots = jnp.zeros((1, BS), F32)
    for at, (i, j) in enumerate(PAIRS):
        dot = jnp.sum(fields[i] * fields[j], axis=(0, 1), keepdims=True)
        dots = jnp.where(lane == at, dot, dots)
    for at in range(out.shape[0]):
        out[at] = dots


def sum_kernel(parts, out):
    total = jnp.sum(parts[...], axis=0)
    for at in range(out.shape[0]):
        out[at] = total


def cholesky(gram, size):
    lower = [[None] * size for _ in range(size)]
    for j in range(size):
        pivot = gram[j][j]
        for k in range(j):
            pivot = pivot - lower[j][k] * lower[j][k]
        lower[j][j] = jnp.sqrt(pivot)
        for i in range(j + 1, size):
            entry = gram[i][j]
            for k in range(j):
                entry = entry - lower[i][k] * lower[j][k]
            lower[i][j] = entry / lower[j][j]
    return lower


def finish_kernel(parts, u0, u1, u2, u3, solution_field, hessenberg):
    total = jnp.sum(parts[...], axis=0)
    lane = lax.broadcasted_iota(jnp.int32, (NB, BS), 1)
    sublane = lax.broadcasted_iota(jnp.int32, (NB, BS), 0)
    total = jnp.broadcast_to(total, (NB, BS))
    size = ITERS + 1
    gram = [[None] * size for _ in range(size)]
    for at, (i, j) in enumerate(PAIRS):
        entry = jnp.sum(jnp.where(lane == at, total, 0.0), axis=1, keepdims=True)
        gram[i][j] = gram[j][i] = jnp.broadcast_to(entry, (NB, BS))
    lower = cholesky(gram, size)
    h = [[None] * ITERS for _ in range(size)]
    for j in range(ITERS):
        for i in range(j + 2):
            entry = lower[j + 1][i]
            if i <= j:
                entry = entry + SHIFT * lower[j][i]
            for k in range(max(i - 1, 0), j):
                entry = entry - h[i][k] * lower[j][k]
            h[i][j] = entry / lower[j][j]
    normal = [[None] * ITERS for _ in range(ITERS)]
    for i in range(ITERS):
        for j in range(i + 1):
            entry = h[0][i] * h[0][j]
            for k in range(1, j + 2):
                entry = entry + h[k][i] * h[k][j]
            normal[i][j] = entry
    factor = cholesky(normal, ITERS)
    forward = []
    for i in range(ITERS):
        entry = lower[0][0] * h[0][i]
        for k in range(i):
            entry = entry - factor[i][k] * forward[k]
        forward.append(entry / factor[i][i])
    y = [None] * ITERS
    for i in reversed(range(ITERS)):
        entry = forward[i]
        for k in range(i + 1, ITERS):
            entry = entry - factor[k][i] * y[k]
        y[i] = entry / factor[i][i]
    weights = [None] * ITERS
    for i in reversed(range(ITERS)):
        entry = y[i]
        for k in range(i + 1, ITERS):
            entry = entry - lower[k][i] * weights[k]
        weights[i] = entry / lower[i][i]
    solution_field[...] = (weights[0] * u0[...] + weights[1] * u1[...]) + (
        weights[2] * u2[...] + weights[3] * u3[...]
    )
    matrix = jnp.zeros((NB, BS), F32)
    for j in range(ITERS):
        for i in range(j + 2):
            matrix = jnp.where((sublane == i) & (lane == j), h[i][j], matrix)
    hessenberg[...] = matrix[:size, :ITERS]


SMEM = pl.BlockSpec(memory_space=pltpu.SMEM)
VMEM = pl.BlockSpec(memory_space=pltpu.VMEM)
FIELD = jax.ShapeDtypeStruct((NB, BS), F32)


def halo_index(block_columns, live_slots):
    where = block_columns.reshape(NB, SLOTS)
    live = lax.broadcasted_iota(jnp.int32, (NB, SLOTS), 1) < live_slots.reshape(NB, 1)

    def side(offset, position):
        forward = jnp.where(position % 2 == 0, 1, 2)
        return jnp.where(offset == 1, 0, jnp.where(offset == 2, forward, 3 - forward))

    row = side(where // (3 * NB), lax.axis_index(ROW))
    col = side(where // NB % 3, lax.axis_index(COL))
    return jnp.where(live, (col * 3 + row) * NB + where % NB, 9 * NB).reshape(-1)


def on_device(rows, cols, right_side, block_values, block_columns, live_slots, row_scale):
    u0 = right_side.reshape(NB, BS)
    values = block_values.reshape(NB * SLOTS, BS, BS)
    scale = row_scale.reshape(NB, BS)
    index = halo_index(block_columns, live_slots)
    halo = [pltpu.VMEM((10 * NB, BS), F32)]

    def apply(field, fine):
        return pl.pallas_call(
            lambda *refs: apply_kernel(fine, *refs),
            out_shape=FIELD,
            in_specs=[SMEM] + [VMEM] * 5,
            out_specs=VMEM,
            scratch_shapes=halo,
        )(index, *exchange(field, rows, cols), values, scale)

    u1 = apply(u0, False)
    u2 = apply(u1, True)
    u3 = apply(u2, True)
    plane = lax.axis_size(PLANE)
    depth = lax.axis_size("z")
    parts = pl.pallas_call(
        last_kernel,
        out_shape=jax.ShapeDtypeStruct((plane, 1, BS), F32),
        in_specs=[SMEM] + [VMEM] * 8,
        out_specs=VMEM,
        scratch_shapes=halo,
    )(index, *exchange(u3, rows, cols), values, scale, u0, u1, u2)
    parts = lax.all_to_all(parts, PLANE, split_axis=0, concat_axis=0, tiled=True)
    parts = pl.pallas_call(
        sum_kernel,
        out_shape=jax.ShapeDtypeStruct((depth, 1, BS), F32),
        in_specs=[VMEM],
        out_specs=VMEM,
    )(parts)
    parts = lax.all_to_all(parts, "z", split_axis=0, concat_axis=0, tiled=True)
    solution_field, hessenberg = pl.pallas_call(
        finish_kernel,
        out_shape=(FIELD, jax.ShapeDtypeStruct((ITERS + 1, ITERS), F32)),
        in_specs=[VMEM] * 5,
        out_specs=(VMEM, VMEM),
    )(parts, u0, u1, u2, u3)
    return solution_field.reshape(right_side.shape), hessenberg


def solution(mesh):
    rows, cols = mesh.shape["row"], mesh.shape["col"]
    finer = Mesh(
        mesh.devices.reshape(4, rows // 4, cols // 2, 2), ("y", "z", "x", "core")
    )
    in_specs = (
        P(ROW, COL, None, None),
        P(ROW, COL, None, None, None, None),
        P(ROW, COL, None, None),
        P(ROW, COL, None),
        P(ROW, COL, None, None),
    )
    out_specs = (P(ROW, COL, None, None), P())
    return jax.shard_map(
        lambda *arrays: on_device(rows, cols, *arrays),
        mesh=finer,
        in_specs=in_specs,
        out_specs=out_specs,
        check_vma=False,
    )
```

```python
import jax
import jax.numpy as jnp
from jax import lax
from jax.experimental import pallas as pl
from jax.experimental.pallas import tpu as pltpu
from jax.sharding import Mesh
from jax.sharding import PartitionSpec as P

ITERS = 4
NB = 8
BS = 128
SLOTS = 4
ROW = ("y", "z")
COL = ("x", "core")
PLANE = ("y", "x", "core")
SHIFT = 2.2
PAIRS = [(i, j) for j in range(ITERS + 1) for i in range(j + 1)]
F32 = jnp.float32
BF16 = jnp.bfloat16


def swaps(count):
    even = [(i, i ^ 1) for i in range(count)]
    odd = []
    for i in range(1, count - 1, 2):
        odd += [(i, i + 1), (i + 1, i)]
    return even, odd


def exchange(field, rows, cols):
    even, odd = swaps(rows)
    beside = jnp.stack(
        [field, lax.ppermute(field, ROW, even), lax.ppermute(field, ROW, odd)]
    )
    even, odd = swaps(cols)
    return (
        beside,
        lax.ppermute(beside, COL, even),
        lax.ppermute(beside, COL, odd),
    )


def fill(halo, parts):
    for at, part in enumerate(parts):
        for row in range(3):
            halo[pl.ds((at * 3 + row) * NB, NB), :] = part[row]
    halo[pl.ds(9 * NB, NB), :] = jnp.zeros((NB, BS), F32)


def multiply(index, halo, values, fine):
    sublane = lax.broadcasted_iota(jnp.int32, (NB, BS), 0)
    total = jnp.zeros((2 * NB, BS), F32)
    for n in range(NB):
        pieces = []
        for s in range(SLOTS):
            row = halo[pl.ds(index[n * SLOTS + s], 1), :]
            row = jnp.where(sublane == n, jnp.broadcast_to(row, (NB, BS)), 0.0)
            high = row.astype(BF16).astype(F32)
            low = row - high if fine else jnp.zeros_like(row)
            pieces.append(jnp.concatenate([high, low], axis=0).astype(BF16))
        left = jnp.concatenate(pieces, axis=1)
        right = jnp.concatenate([values[n * SLOTS + s] for s in range(SLOTS)], axis=1)
        total = total + lax.dot_general(
            left, right, (((1,), (1,)), ((), ())), preferred_element_type=F32
        )
    return total[:NB] + total[NB:]


def apply_kernel(fine, index, own, even, odd, values, scale, out, halo):
    fill(halo, (own, even, odd))
    field = own[0]
    product = multiply(index, halo, values, fine)
    out[...] = (scale[...] * field - SHIFT * field) + product


def last_kernel(index, own, even, odd, values, scale, u0, u1, u2, out, halo):
    fill(halo, (own, even, odd))
    field = own[0]
    product = multiply(index, halo, values, True)
    u4 = (scale[...] * field - SHIFT * field) + product
    fields = (u0[...], u1[...], u2[...], field, u4)
    lane = lax.broadcasted_iota(jnp.int32, (1, BS), 1)
    dots = jnp.zeros((1, BS), F32)
    for at, (i, j) in enumerate(PAIRS):
        dot = jnp.sum(fields[i] * fields[j], axis=(0, 1), keepdims=True)
        dots = jnp.where(lane == at, dot, dots)
    for at in range(out.shape[0]):
        out[at] = dots


def sum_kernel(parts, out):
    total = jnp.sum(parts[...], axis=0)
    for at in range(out.shape[0]):
        out[at] = total


def cholesky(gram, size):
    lower = [[None] * size for _ in range(size)]
    for j in range(size):
        pivot = gram[j][j]
        for k in range(j):
            pivot = pivot - lower[j][k] * lower[j][k]
        lower[j][j] = jnp.sqrt(pivot)
        for i in range(j + 1, size):
            entry = gram[i][j]
            for k in range(j):
                entry = entry - lower[i][k] * lower[j][k]
            lower[i][j] = entry / lower[j][j]
    return lower


def finish_kernel(parts, u0, u1, u2, u3, solution_field, hessenberg):
    total = jnp.sum(parts[...], axis=0)
    lane = lax.broadcasted_iota(jnp.int32, (NB, BS), 1)
    sublane = lax.broadcasted_iota(jnp.int32, (NB, BS), 0)
    total = jnp.broadcast_to(total, (NB, BS))
    size = ITERS + 1
    gram = [[None] * size for _ in range(size)]
    for at, (i, j) in enumerate(PAIRS):
        entry = jnp.sum(jnp.where(lane == at, total, 0.0), axis=1, keepdims=True)
        gram[i][j] = gram[j][i] = jnp.broadcast_to(entry, (NB, BS))
    lower = cholesky(gram, size)
    h = [[None] * ITERS for _ in range(size)]
    for j in range(ITERS):
        for i in range(j + 2):
            entry = lower[j + 1][i]
            if i <= j:
                entry = entry + SHIFT * lower[j][i]
            for k in range(max(i - 1, 0), j):
                entry = entry - h[i][k] * lower[j][k]
            h[i][j] = entry / lower[j][j]
    normal = [[None] * ITERS for _ in range(ITERS)]
    for i in range(ITERS):
        for j in range(i + 1):
            entry = h[0][i] * h[0][j]
            for k in range(1, j + 2):
                entry = entry + h[k][i] * h[k][j]
            normal[i][j] = entry
    factor = cholesky(normal, ITERS)
    forward = []
    for i in range(ITERS):
        entry = lower[0][0] * h[0][i]
        for k in range(i):
            entry = entry - factor[i][k] * forward[k]
        forward.append(entry / factor[i][i])
    y = [None] * ITERS
    for i in reversed(range(ITERS)):
        entry = forward[i]
        for k in range(i + 1, ITERS):
            entry = entry - factor[k][i] * y[k]
        y[i] = entry / factor[i][i]
    weights = [None] * ITERS
    for i in reversed(range(ITERS)):
        entry = y[i]
        for k in range(i + 1, ITERS):
            entry = entry - lower[k][i] * weights[k]
        weights[i] = entry / lower[i][i]
    solution_field[...] = (weights[0] * u0[...] + weights[1] * u1[...]) + (
        weights[2] * u2[...] + weights[3] * u3[...]
    )
    matrix = jnp.zeros((NB, BS), F32)
    for j in range(ITERS):
        for i in range(j + 2):
            matrix = jnp.where((sublane == j) & (lane == i), h[i][j], matrix)
    hessenberg[...] = matrix[:ITERS, :size]


SMEM = pl.BlockSpec(memory_space=pltpu.SMEM)
VMEM = pl.BlockSpec(memory_space=pltpu.VMEM)
PARAMS = pltpu.CompilerParams(vmem_limit_bytes=4 << 20)
FIELD = jax.ShapeDtypeStruct((NB, BS), F32)


def halo_index(block_columns, live_slots):
    where = block_columns.reshape(NB, SLOTS)
    live = lax.broadcasted_iota(jnp.int32, (NB, SLOTS), 1) < live_slots.reshape(NB, 1)

    def side(offset, position):
        forward = jnp.where(position % 2 == 0, 1, 2)
        return jnp.where(offset == 1, 0, jnp.where(offset == 2, forward, 3 - forward))

    row = side(where // (3 * NB), lax.axis_index(ROW))
    col = side(where // NB % 3, lax.axis_index(COL))
    return jnp.where(live, (col * 3 + row) * NB + where % NB, 9 * NB).reshape(-1)


def on_device(rows, cols, right_side, block_values, block_columns, live_slots, row_scale):
    u0 = right_side.reshape(NB, BS)
    values = block_values.reshape(NB * SLOTS, BS, BS)
    scale = row_scale.reshape(NB, BS)
    index = halo_index(block_columns, live_slots)
    halo = [pltpu.VMEM((10 * NB, BS), F32)]

    def apply(field, fine):
        return pl.pallas_call(
            lambda *refs: apply_kernel(fine, *refs),
            out_shape=FIELD,
            in_specs=[SMEM] + [VMEM] * 5,
            out_specs=VMEM,
            scratch_shapes=halo,
            compiler_params=PARAMS,
        )(index, *exchange(field, rows, cols), values, scale)

    u1 = apply(u0, False)
    u2 = apply(u1, True)
    u3 = apply(u2, True)
    plane = lax.axis_size(PLANE)
    depth = lax.axis_size("z")
    parts = pl.pallas_call(
        last_kernel,
        out_shape=jax.ShapeDtypeStruct((plane, 1, BS), F32),
        in_specs=[SMEM] + [VMEM] * 8,
        out_specs=VMEM,
        scratch_shapes=halo,
        compiler_params=PARAMS,
    )(index, *exchange(u3, rows, cols), values, scale, u0, u1, u2)
    parts = lax.all_to_all(parts, PLANE, split_axis=0, concat_axis=0, tiled=True)
    parts = pl.pallas_call(
        sum_kernel,
        out_shape=jax.ShapeDtypeStruct((depth, 1, BS), F32),
        in_specs=[VMEM],
        out_specs=VMEM,
        compiler_params=PARAMS,
    )(parts)
    parts = lax.all_to_all(parts, "z", split_axis=0, concat_axis=0, tiled=True)
    solution_field, hessenberg = pl.pallas_call(
        finish_kernel,
        out_shape=(FIELD, jax.ShapeDtypeStruct((ITERS, ITERS + 1), F32)),
        in_specs=[VMEM] * 5,
        out_specs=(VMEM, VMEM),
        compiler_params=PARAMS,
    )(parts, u0, u1, u2, u3)
    return solution_field.reshape(right_side.shape), hessenberg.T


def solution(mesh):
    rows, cols = mesh.shape["row"], mesh.shape["col"]
    finer = Mesh(
        mesh.devices.reshape(4, rows // 4, cols // 2, 2), ("y", "z", "x", "core")
    )
    in_specs = (
        P(ROW, COL, None, None),
        P(ROW, COL, None, None, None, None),
        P(ROW, COL, None, None),
        P(ROW, COL, None),
        P(ROW, COL, None, None),
    )
    out_specs = (P(ROW, COL, None, None), P())
    return jax.shard_map(
        lambda *arrays: on_device(rows, cols, *arrays),
        mesh=finer,
        in_specs=in_specs,
        out_specs=out_specs,
        check_vma=False,
    )
```

```python
import jax
import jax.numpy as jnp
from jax import lax
from jax.experimental import pallas as pl
from jax.experimental.pallas import tpu as pltpu
from jax.sharding import Mesh
from jax.sharding import PartitionSpec as P

ITERS = 4
NB = 8
BS = 128
SLOTS = 4
ROW = ("y", "z")
COL = ("x", "core")
PLANE = ("y", "x", "core")
SHIFT = 2.2
PAIRS = [(i, j) for j in range(ITERS + 1) for i in range(j + 1)]
F32 = jnp.float32
BF16 = jnp.bfloat16


def swaps(count):
    even = [(i, i ^ 1) for i in range(count)]
    odd = []
    for i in range(1, count - 1, 2):
        odd += [(i, i + 1), (i + 1, i)]
    return even, odd


def exchange(field, rows, cols):
    even, odd = swaps(cols)
    beside = jnp.stack(
        [field, lax.ppermute(field, COL, even), lax.ppermute(field, COL, odd)]
    )
    even, odd = swaps(rows)
    return (
        beside,
        lax.ppermute(beside, ROW, even),
        lax.ppermute(beside, ROW, odd),
    )


def multiply(pick, parts, values, fine):
    halo = jnp.concatenate([part[...].reshape(3 * NB, BS) for part in parts], axis=0)
    high = halo.astype(BF16).astype(F32)
    halo = jnp.concatenate([high, halo - high], axis=1) if fine else high
    taken = jnp.dot(pick[...], halo.astype(BF16), preferred_element_type=F32)
    sublane = lax.broadcasted_iota(jnp.int32, (NB, BS), 0)
    total = jnp.zeros((2 * NB, BS), F32)
    for n in range(NB):
        left = []
        for s in range(SLOTS):
            rows = [taken[s * NB : (s + 1) * NB, at : at + BS] for at in range(0, taken.shape[1], BS)]
            rows = [jnp.where(sublane == n, row, 0.0) for row in rows]
            rows += [jnp.zeros_like(rows[0])] * (2 - len(rows))
            left.append(jnp.concatenate(rows, axis=0).astype(BF16))
        right = jnp.concatenate([values[n * SLOTS + s] for s in range(SLOTS)], axis=1)
        total = total + lax.dot_general(
            jnp.concatenate(left, axis=1),
            right,
            (((1,), (1,)), ((), ())),
            preferred_element_type=F32,
        )
    return total[:NB] + total[NB:]


def image(pick, own, even, odd, values, scale, fine):
    field = own[0]
    product = multiply(pick, (own, even, odd), values, fine)
    return field, (scale[...] * field - SHIFT * field) + product


def apply_kernel(fine, pick, own, even, odd, values, scale, out):
    out[...] = image(pick, own, even, odd, values, scale, fine)[1]


def last_kernel(pick, own, even, odd, values, scale, u0, u1, u2, out):
    field, u4 = image(pick, own, even, odd, values, scale, True)
    fields = (u0[...], u1[...], u2[...], field, u4)
    lane = lax.broadcasted_iota(jnp.int32, (1, BS), 1)
    dots = jnp.zeros((1, BS), F32)
    for at, (i, j) in enumerate(PAIRS):
        dot = jnp.sum(fields[i] * fields[j], axis=(0, 1), keepdims=True)
        dots = jnp.where(lane == at, dot, dots)
    for at in range(out.shape[0]):
        out[at] = dots


def sum_kernel(parts, out):
    total = jnp.sum(parts[...], axis=0)
    for at in range(out.shape[0]):
        out[at] = total


def fetch_kernel(source, out, arrived):
    copy = pltpu.make_async_copy(source, out, arrived)
    copy.start()
    copy.wait()


def cholesky(gram, size):
    lower = [[None] * size for _ in range(size)]
    for j in range(size):
        pivot = gram[j][j]
        for k in range(j):
            pivot = pivot - lower[j][k] * lower[j][k]
        lower[j][j] = jnp.sqrt(pivot)
        for i in range(j + 1, size):
            entry = gram[i][j]
            for k in range(j):
                entry = entry - lower[i][k] * lower[j][k]
            lower[i][j] = entry / lower[j][j]
    return lower


def finish_kernel(parts, u0, u1, u2, u3, solution_field, hessenberg):
    total = jnp.sum(parts[...], axis=0)
    lane = lax.broadcasted_iota(jnp.int32, (NB, BS), 1)
    sublane = lax.broadcasted_iota(jnp.int32, (NB, BS), 0)
    total = jnp.broadcast_to(total, (NB, BS))
    size = ITERS + 1
    gram = [[None] * size for _ in range(size)]
    for at, (i, j) in enumerate(PAIRS):
        entry = jnp.sum(jnp.where(lane == at, total, 0.0), axis=1, keepdims=True)
        gram[i][j] = gram[j][i] = jnp.broadcast_to(entry, (NB, BS))
    lower = cholesky(gram, size)
    h = [[None] * ITERS for _ in range(size)]
    for j in range(ITERS):
        for i in range(j + 2):
            entry = lower[j + 1][i]
            if i <= j:
                entry = entry + SHIFT * lower[j][i]
            for k in range(max(i - 1, 0), j):
                entry = entry - h[i][k] * lower[j][k]
            h[i][j] = entry / lower[j][j]
    normal = [[None] * ITERS for _ in range(ITERS)]
    for i in range(ITERS):
        for j in range(i + 1):
            entry = h[0][i] * h[0][j]
            for k in range(1, j + 2):
                entry = entry + h[k][i] * h[k][j]
            normal[i][j] = entry
    factor = cholesky(normal, ITERS)
    forward = []
    for i in range(ITERS):
        entry = lower[0][0] * h[0][i]
        for k in range(i):
            entry = entry - factor[i][k] * forward[k]
        forward.append(entry / factor[i][i])
    y = [None] * ITERS
    for i in reversed(range(ITERS)):
        entry = forward[i]
        for k in range(i + 1, ITERS):
            entry = entry - factor[k][i] * y[k]
        y[i] = entry / factor[i][i]
    weights = [None] * ITERS
    for i in reversed(range(ITERS)):
        entry = y[i]
        for k in range(i + 1, ITERS):
            entry = entry - lower[k][i] * weights[k]
        weights[i] = entry / lower[i][i]
    solution_field[...] = (weights[0] * u0[...] + weights[1] * u1[...]) + (
        weights[2] * u2[...] + weights[3] * u3[...]
    )
    matrix = jnp.zeros((NB, BS), F32)
    for j in range(ITERS):
        for i in range(j + 2):
            matrix = jnp.where((sublane == j) & (lane == i), h[i][j], matrix)
    hessenberg[...] = matrix[:ITERS, :size]


VMEM = pl.BlockSpec(memory_space=pltpu.VMEM)
PARAMS = pltpu.CompilerParams(vmem_limit_bytes=4 << 20)
FIELD = jax.ShapeDtypeStruct((NB, BS), F32)


def slot_picks(block_columns, live_slots):
    where = block_columns.reshape(NB, SLOTS).T
    live = lax.broadcasted_iota(jnp.int32, (SLOTS, NB), 0) < live_slots.reshape(1, NB)

    def side(offset, position):
        forward = jnp.where(position % 2 == 0, 1, 2)
        return jnp.where(offset == 1, 0, jnp.where(offset == 2, forward, 3 - forward))

    row = side(where // (3 * NB), lax.axis_index(ROW))
    col = side(where // NB % 3, lax.axis_index(COL))
    place = jnp.where(live, (row * 3 + col) * NB + where % NB, -1)
    blocks = lax.broadcasted_iota(jnp.int32, (SLOTS, NB, 9 * NB), 2)
    return (place[:, :, None] == blocks).astype(BF16).reshape(SLOTS * NB, 9 * NB)


def on_device(rows, cols, right_side, block_values, block_columns, live_slots, row_scale):
    u0 = right_side.reshape(NB, BS)
    values = block_values.reshape(NB * SLOTS, BS, BS)
    values = pl.pallas_call(
        fetch_kernel,
        out_shape=jax.ShapeDtypeStruct(values.shape, BF16),
        in_specs=[pl.BlockSpec(memory_space=pltpu.HBM)],
        out_specs=VMEM,
        scratch_shapes=[pltpu.SemaphoreType.DMA],
        compiler_params=pltpu.CompilerParams(vmem_limit_bytes=52 << 20),
    )(values)
    scale = row_scale.reshape(NB, BS)
    pick = slot_picks(block_columns, live_slots)

    def apply(field, fine):
        return pl.pallas_call(
            lambda *refs: apply_kernel(fine, *refs),
            out_shape=FIELD,
            in_specs=[VMEM] * 6,
            out_specs=VMEM,
            compiler_params=PARAMS,
        )(pick, *exchange(field, rows, cols), values, scale)

    u1 = apply(u0, False)
    u2 = apply(u1, True)
    u3 = apply(u2, True)
    plane = lax.axis_size(PLANE)
    depth = lax.axis_size("z")
    parts = pl.pallas_call(
        last_kernel,
        out_shape=jax.ShapeDtypeStruct((plane, 1, BS), F32),
        in_specs=[VMEM] * 9,
        out_specs=VMEM,
        compiler_params=PARAMS,
    )(pick, *exchange(u3, rows, cols), values, scale, u0, u1, u2)
    parts = lax.all_to_all(parts, PLANE, split_axis=0, concat_axis=0, tiled=True)
    parts = pl.pallas_call(
        sum_kernel,
        out_shape=jax.ShapeDtypeStruct((depth, 1, BS), F32),
        in_specs=[VMEM],
        out_specs=VMEM,
        compiler_params=PARAMS,
    )(parts)
    parts = lax.all_to_all(parts, "z", split_axis=0, concat_axis=0, tiled=True)
    solution_field, hessenberg = pl.pallas_call(
        finish_kernel,
        out_shape=(FIELD, jax.ShapeDtypeStruct((ITERS, ITERS + 1), F32)),
        in_specs=[VMEM] * 5,
        out_specs=(VMEM, VMEM),
        compiler_params=PARAMS,
    )(parts, u0, u1, u2, u3)
    return solution_field.reshape(right_side.shape), hessenberg.T


def solution(mesh):
    rows, cols = mesh.shape["row"], mesh.shape["col"]
    finer = Mesh(
        mesh.devices.reshape(4, rows // 4, cols // 2, 2), ("y", "z", "x", "core")
    )
    in_specs = (
        P(ROW, COL, None, None),
        P(ROW, COL, None, None, None, None),
        P(ROW, COL, None, None),
        P(ROW, COL, None),
        P(ROW, COL, None, None),
    )
    out_specs = (P(ROW, COL, None, None), P())
    return jax.shard_map(
        lambda *arrays: on_device(rows, cols, *arrays),
        mesh=finer,
        in_specs=in_specs,
        out_specs=out_specs,
        check_vma=False,
    )
```

```python
import jax
import jax.numpy as jnp
from jax import lax
from jax.experimental import pallas as pl
from jax.experimental.pallas import tpu as pltpu
from jax.sharding import Mesh
from jax.sharding import PartitionSpec as P

ITERS = 4
NB = 8
BS = 128
SLOTS = 4
ROW = ("y", "z")
COL = ("x", "core")
PLANE = ("y", "x", "core")
SHIFT = 2.2
PAIRS = [(i, j) for j in range(ITERS + 1) for i in range(j + 1)]
F32 = jnp.float32
BF16 = jnp.bfloat16


def swaps(count):
    even = [(i, i ^ 1) for i in range(count)]
    odd = []
    for i in range(1, count - 1, 2):
        odd += [(i, i + 1), (i + 1, i)]
    return even, odd


def exchange(field, rows, cols):
    even, odd = swaps(cols)
    beside = jnp.stack(
        [field, lax.ppermute(field, COL, even), lax.ppermute(field, COL, odd)]
    )
    even, odd = swaps(rows)
    return (
        beside,
        lax.ppermute(beside, ROW, even),
        lax.ppermute(beside, ROW, odd),
    )


def multiply(pick, parts, values, fine):
    halo = jnp.concatenate([part[...].reshape(3 * NB, BS) for part in parts], axis=0)
    high = halo.astype(BF16).astype(F32)
    halo = jnp.concatenate([high, halo - high], axis=1) if fine else high
    taken = jnp.dot(pick[...], halo.astype(BF16), preferred_element_type=F32)
    sublane = lax.broadcasted_iota(jnp.int32, (NB, BS), 0)
    total = jnp.zeros((2 * NB, BS), F32)
    for n in range(NB):
        left = []
        for s in range(SLOTS):
            rows = [taken[s * NB : (s + 1) * NB, at : at + BS] for at in range(0, taken.shape[1], BS)]
            rows = [jnp.where(sublane == n, row, 0.0) for row in rows]
            rows += [jnp.zeros_like(rows[0])] * (2 - len(rows))
            left.append(jnp.concatenate(rows, axis=0).astype(BF16))
        right = jnp.concatenate([values[n * SLOTS + s] for s in range(SLOTS)], axis=0)
        total = total + jnp.dot(
            jnp.concatenate(left, axis=1), right, preferred_element_type=F32
        )
    return total[:NB] + total[NB:]


def image(pick, own, even, odd, values, scale, fine):
    field = own[0]
    product = multiply(pick, (own, even, odd), values, fine)
    return field, (scale[...] * field - SHIFT * field) + product


def apply_kernel(fine, pick, own, even, odd, values, scale, out):
    out[...] = image(pick, own, even, odd, values, scale, fine)[1]


def last_kernel(pick, own, even, odd, values, scale, u0, u1, u2, out):
    field, u4 = image(pick, own, even, odd, values, scale, True)
    fields = (u0[...], u1[...], u2[...], field, u4)
    lane = lax.broadcasted_iota(jnp.int32, (1, BS), 1)
    dots = jnp.zeros((1, BS), F32)
    for at, (i, j) in enumerate(PAIRS):
        dot = jnp.sum(fields[i] * fields[j], axis=(0, 1), keepdims=True)
        dots = jnp.where(lane == at, dot, dots)
    for at in range(out.shape[0]):
        out[at] = dots


def sum_kernel(parts, out):
    total = jnp.sum(parts[...], axis=0)
    for at in range(out.shape[0]):
        out[at] = total


def fetch_kernel(source, out, landed, arrived):
    copies = [
        pltpu.make_async_copy(
            source.at[pl.ds(n * SLOTS, SLOTS)], landed.at[pl.ds(n * SLOTS, SLOTS)], arrived.at[n]
        )
        for n in range(NB)
    ]
    for copy in copies:
        copy.start()
    for n in range(NB):
        copies[n].wait()
        for s in range(SLOTS):
            out[n * SLOTS + s] = landed[n * SLOTS + s].T


def cholesky(gram, size):
    lower = [[None] * size for _ in range(size)]
    for j in range(size):
        pivot = gram[j][j]
        for k in range(j):
            pivot = pivot - lower[j][k] * lower[j][k]
        lower[j][j] = jnp.sqrt(pivot)
        for i in range(j + 1, size):
            entry = gram[i][j]
            for k in range(j):
                entry = entry - lower[i][k] * lower[j][k]
            lower[i][j] = entry / lower[j][j]
    return lower


def finish_kernel(parts, u0, u1, u2, u3, solution_field, hessenberg):
    total = jnp.sum(parts[...], axis=0)
    lane = lax.broadcasted_iota(jnp.int32, (NB, BS), 1)
    sublane = lax.broadcasted_iota(jnp.int32, (NB, BS), 0)
    total = jnp.broadcast_to(total, (NB, BS))
    size = ITERS + 1
    gram = [[None] * size for _ in range(size)]
    for at, (i, j) in enumerate(PAIRS):
        entry = jnp.sum(jnp.where(lane == at, total, 0.0), axis=1, keepdims=True)
        gram[i][j] = gram[j][i] = jnp.broadcast_to(entry, (NB, BS))
    lower = cholesky(gram, size)
    h = [[None] * ITERS for _ in range(size)]
    for j in range(ITERS):
        for i in range(j + 2):
            entry = lower[j + 1][i]
            if i <= j:
                entry = entry + SHIFT * lower[j][i]
            for k in range(max(i - 1, 0), j):
                entry = entry - h[i][k] * lower[j][k]
            h[i][j] = entry / lower[j][j]
    normal = [[None] * ITERS for _ in range(ITERS)]
    for i in range(ITERS):
        for j in range(i + 1):
            entry = h[0][i] * h[0][j]
            for k in range(1, j + 2):
                entry = entry + h[k][i] * h[k][j]
            normal[i][j] = entry
    factor = cholesky(normal, ITERS)
    forward = []
    for i in range(ITERS):
        entry = lower[0][0] * h[0][i]
        for k in range(i):
            entry = entry - factor[i][k] * forward[k]
        forward.append(entry / factor[i][i])
    y = [None] * ITERS
    for i in reversed(range(ITERS)):
        entry = forward[i]
        for k in range(i + 1, ITERS):
            entry = entry - factor[k][i] * y[k]
        y[i] = entry / factor[i][i]
    weights = [None] * ITERS
    for i in reversed(range(ITERS)):
        entry = y[i]
        for k in range(i + 1, ITERS):
            entry = entry - lower[k][i] * weights[k]
        weights[i] = entry / lower[i][i]
    solution_field[...] = (weights[0] * u0[...] + weights[1] * u1[...]) + (
        weights[2] * u2[...] + weights[3] * u3[...]
    )
    matrix = jnp.zeros((NB, BS), F32)
    for j in range(ITERS):
        for i in range(j + 2):
            matrix = jnp.where((sublane == j) & (lane == i), h[i][j], matrix)
    hessenberg[...] = matrix[:ITERS, :size]


VMEM = pl.BlockSpec(memory_space=pltpu.VMEM)
PARAMS = pltpu.CompilerParams(vmem_limit_bytes=4 << 20)
FIELD = jax.ShapeDtypeStruct((NB, BS), F32)


def slot_picks(block_columns, live_slots):
    where = block_columns.reshape(NB, SLOTS).T
    live = lax.broadcasted_iota(jnp.int32, (SLOTS, NB), 0) < live_slots.reshape(1, NB)

    def side(offset, position):
        forward = jnp.where(position % 2 == 0, 1, 2)
        return jnp.where(offset == 1, 0, jnp.where(offset == 2, forward, 3 - forward))

    row = side(where // (3 * NB), lax.axis_index(ROW))
    col = side(where // NB % 3, lax.axis_index(COL))
    place = jnp.where(live, (row * 3 + col) * NB + where % NB, -1)
    blocks = lax.broadcasted_iota(jnp.int32, (SLOTS, NB, 9 * NB), 2)
    return (place[:, :, None] == blocks).astype(BF16).reshape(SLOTS * NB, 9 * NB)


def on_device(rows, cols, right_side, block_values, block_columns, live_slots, row_scale):
    u0 = right_side.reshape(NB, BS)
    values = block_values.reshape(NB * SLOTS, BS, BS)
    values = pl.pallas_call(
        fetch_kernel,
        out_shape=jax.ShapeDtypeStruct(values.shape, BF16),
        in_specs=[pl.BlockSpec(memory_space=pltpu.HBM)],
        out_specs=VMEM,
        scratch_shapes=[
            pltpu.VMEM(values.shape, BF16),
            pltpu.SemaphoreType.DMA((NB,)),
        ],
        compiler_params=pltpu.CompilerParams(vmem_limit_bytes=52 << 20),
    )(values)
    scale = row_scale.reshape(NB, BS)
    pick = slot_picks(block_columns, live_slots)

    def apply(field, fine):
        return pl.pallas_call(
            lambda *refs: apply_kernel(fine, *refs),
            out_shape=FIELD,
            in_specs=[VMEM] * 6,
            out_specs=VMEM,
            compiler_params=PARAMS,
        )(pick, *exchange(field, rows, cols), values, scale)

    u1 = apply(u0, False)
    u2 = apply(u1, True)
    u3 = apply(u2, True)
    plane = lax.axis_size(PLANE)
    depth = lax.axis_size("z")
    parts = pl.pallas_call(
        last_kernel,
        out_shape=jax.ShapeDtypeStruct((plane, 1, BS), F32),
        in_specs=[VMEM] * 9,
        out_specs=VMEM,
        compiler_params=PARAMS,
    )(pick, *exchange(u3, rows, cols), values, scale, u0, u1, u2)
    parts = lax.all_to_all(parts, PLANE, split_axis=0, concat_axis=0, tiled=True)
    parts = pl.pallas_call(
        sum_kernel,
        out_shape=jax.ShapeDtypeStruct((depth, 1, BS), F32),
        in_specs=[VMEM],
        out_specs=VMEM,
        compiler_params=PARAMS,
    )(parts)
    parts = lax.all_to_all(parts, "z", split_axis=0, concat_axis=0, tiled=True)
    solution_field, hessenberg = pl.pallas_call(
        finish_kernel,
        out_shape=(FIELD, jax.ShapeDtypeStruct((ITERS, ITERS + 1), F32)),
        in_specs=[VMEM] * 5,
        out_specs=(VMEM, VMEM),
        compiler_params=PARAMS,
    )(parts, u0, u1, u2, u3)
    return solution_field.reshape(right_side.shape), hessenberg.T


def solution(mesh):
    rows, cols = mesh.shape["row"], mesh.shape["col"]
    finer = Mesh(
        mesh.devices.reshape(4, rows // 4, cols // 2, 2), ("y", "z", "x", "core")
    )
    in_specs = (
        P(ROW, COL, None, None),
        P(ROW, COL, None, None, None, None),
        P(ROW, COL, None, None),
        P(ROW, COL, None),
        P(ROW, COL, None, None),
    )
    out_specs = (P(ROW, COL, None, None), P())
    return jax.shard_map(
        lambda *arrays: on_device(rows, cols, *arrays),
        mesh=finer,
        in_specs=in_specs,
        out_specs=out_specs,
        check_vma=False,
    )
```

```python
import jax
import jax.numpy as jnp
from jax import lax
from jax.experimental import pallas as pl
from jax.experimental.pallas import tpu as pltpu
from jax.sharding import Mesh
from jax.sharding import PartitionSpec as P

ITERS = 4
NB = 8
BS = 128
SLOTS = 4
ROW = ("y", "z")
COL = ("x", "core")
PLANE = ("core", "x", "y")
SHIFT = 2.2
PAIRS = [(i, j) for j in range(ITERS + 1) for i in range(j + 1)]
F32 = jnp.float32
BF16 = jnp.bfloat16


def swaps(count):
    even = [(i, i ^ 1) for i in range(count)]
    odd = []
    for i in range(1, count - 1, 2):
        odd += [(i, i + 1), (i + 1, i)]
    return even, odd


def exchange(field, rows, cols):
    even, odd = swaps(cols)
    beside = jnp.stack(
        [field, lax.ppermute(field, COL, even), lax.ppermute(field, COL, odd)]
    )
    even, odd = swaps(rows)
    return (
        beside,
        lax.ppermute(beside, ROW, even),
        lax.ppermute(beside, ROW, odd),
    )


def multiply(pick, parts, values, fine):
    halo = jnp.concatenate([part[...].reshape(3 * NB, BS) for part in parts], axis=0)
    high = halo.astype(BF16).astype(F32)
    halo = jnp.concatenate([high, halo - high], axis=1) if fine else high
    taken = jnp.dot(pick[...], halo.astype(BF16), preferred_element_type=F32)
    sublane = lax.broadcasted_iota(jnp.int32, (NB, BS), 0)
    total = jnp.zeros((2 * NB, BS), F32)
    for n in range(NB):
        left = []
        for s in range(SLOTS):
            rows = [taken[s * NB : (s + 1) * NB, at : at + BS] for at in range(0, taken.shape[1], BS)]
            rows = [jnp.where(sublane == n, row, 0.0) for row in rows]
            rows += [jnp.zeros_like(rows[0])] * (2 - len(rows))
            left.append(jnp.concatenate(rows, axis=0).astype(BF16))
        right = jnp.concatenate([values[n * SLOTS + s] for s in range(SLOTS)], axis=0)
        total = total + jnp.dot(
            jnp.concatenate(left, axis=1), right, preferred_element_type=F32
        )
    return total[:NB] + total[NB:]


def image(pick, own, even, odd, values, scale, fine):
    field = own[0]
    product = multiply(pick, (own, even, odd), values, fine)
    return field, (scale[...] * field - SHIFT * field) + product


def apply_kernel(fine, pick, own, even, odd, values, scale, out):
    out[...] = image(pick, own, even, odd, values, scale, fine)[1]


def last_kernel(pick, own, even, odd, values, scale, u0, u1, u2, out):
    field, u4 = image(pick, own, even, odd, values, scale, True)
    fields = (u0[...], u1[...], u2[...], field, u4)
    lane = lax.broadcasted_iota(jnp.int32, (1, BS), 1)
    dots = jnp.zeros((1, BS), F32)
    for at, (i, j) in enumerate(PAIRS):
        dot = jnp.sum(fields[i] * fields[j], axis=(0, 1), keepdims=True)
        dots = jnp.where(lane == at, dot, dots)
    for at in range(out.shape[0]):
        out[at] = dots


def sum_kernel(parts, out):
    total = jnp.sum(parts[...], axis=0)
    for at in range(out.shape[0]):
        out[at] = total


def fetch_kernel(source, out, landed, arrived):
    copies = [
        pltpu.make_async_copy(
            source.at[pl.ds(n * SLOTS, SLOTS)], landed.at[pl.ds(n * SLOTS, SLOTS)], arrived.at[n]
        )
        for n in range(NB)
    ]
    for copy in copies:
        copy.start()
    for n in range(NB):
        copies[n].wait()
        for s in range(SLOTS):
            out[n * SLOTS + s] = landed[n * SLOTS + s].T


def cholesky(gram, size):
    lower = [[None] * size for _ in range(size)]
    inverse = []
    for j in range(size):
        pivot = gram[j][j]
        for k in range(j):
            pivot = pivot - lower[j][k] * lower[j][k]
        lower[j][j] = jnp.sqrt(pivot)
        inverse.append(1.0 / lower[j][j])
        for i in range(j + 1, size):
            entry = gram[i][j]
            for k in range(j):
                entry = entry - lower[i][k] * lower[j][k]
            lower[i][j] = entry * inverse[j]
    return lower, inverse


def finish_kernel(parts, u0, u1, u2, u3, solution_field, hessenberg):
    total = jnp.sum(parts[...], axis=0)
    lane = lax.broadcasted_iota(jnp.int32, (NB, BS), 1)
    sublane = lax.broadcasted_iota(jnp.int32, (NB, BS), 0)
    total = jnp.broadcast_to(total, (NB, BS))
    size = ITERS + 1
    gram = [[None] * size for _ in range(size)]
    for at, (i, j) in enumerate(PAIRS):
        entry = jnp.sum(jnp.where(lane == at, total, 0.0), axis=1, keepdims=True)
        gram[i][j] = gram[j][i] = jnp.broadcast_to(entry, (NB, BS))
    lower, inverse = cholesky(gram, size)
    h = [[None] * ITERS for _ in range(size)]
    for j in range(ITERS):
        for i in range(j + 2):
            entry = lower[j + 1][i]
            if i <= j:
                entry = entry + SHIFT * lower[j][i]
            for k in range(max(i - 1, 0), j):
                entry = entry - h[i][k] * lower[j][k]
            h[i][j] = entry * inverse[j]
    normal = [[None] * ITERS for _ in range(ITERS)]
    for i in range(ITERS):
        for j in range(i + 1):
            entry = h[0][i] * h[0][j]
            for k in range(1, j + 2):
                entry = entry + h[k][i] * h[k][j]
            normal[i][j] = entry
    factor, scaled = cholesky(normal, ITERS)
    forward = []
    for i in range(ITERS):
        entry = lower[0][0] * h[0][i]
        for k in range(i):
            entry = entry - factor[i][k] * forward[k]
        forward.append(entry * scaled[i])
    y = [None] * ITERS
    for i in reversed(range(ITERS)):
        entry = forward[i]
        for k in range(i + 1, ITERS):
            entry = entry - factor[k][i] * y[k]
        y[i] = entry * scaled[i]
    weights = [None] * ITERS
    for i in reversed(range(ITERS)):
        entry = y[i]
        for k in range(i + 1, ITERS):
            entry = entry - lower[k][i] * weights[k]
        weights[i] = entry * inverse[i]
    solution_field[...] = (weights[0] * u0[...] + weights[1] * u1[...]) + (
        weights[2] * u2[...] + weights[3] * u3[...]
    )
    matrix = jnp.zeros((NB, BS), F32)
    for j in range(ITERS):
        for i in range(j + 2):
            matrix = jnp.where((sublane == j) & (lane == i), h[i][j], matrix)
    hessenberg[...] = matrix[:ITERS, :size]


VMEM = pl.BlockSpec(memory_space=pltpu.VMEM)
PARAMS = pltpu.CompilerParams(vmem_limit_bytes=4 << 20)
FIELD = jax.ShapeDtypeStruct((NB, BS), F32)


def slot_picks(block_columns, live_slots):
    where = block_columns.reshape(NB, SLOTS).T
    live = lax.broadcasted_iota(jnp.int32, (SLOTS, NB), 0) < live_slots.reshape(1, NB)

    def side(offset, position):
        forward = jnp.where(position % 2 == 0, 1, 2)
        return jnp.where(offset == 1, 0, jnp.where(offset == 2, forward, 3 - forward))

    row = side(where // (3 * NB), lax.axis_index(ROW))
    col = side(where // NB % 3, lax.axis_index(COL))
    place = jnp.where(live, (row * 3 + col) * NB + where % NB, -1)
    blocks = lax.broadcasted_iota(jnp.int32, (SLOTS, NB, 9 * NB), 2)
    return (place[:, :, None] == blocks).astype(BF16).reshape(SLOTS * NB, 9 * NB)


def on_device(rows, cols, right_side, block_values, block_columns, live_slots, row_scale):
    u0 = right_side.reshape(NB, BS)
    values = block_values.reshape(NB * SLOTS, BS, BS)
    values = pl.pallas_call(
        fetch_kernel,
        out_shape=jax.ShapeDtypeStruct(values.shape, BF16),
        in_specs=[pl.BlockSpec(memory_space=pltpu.HBM)],
        out_specs=VMEM,
        scratch_shapes=[
            pltpu.VMEM(values.shape, BF16),
            pltpu.SemaphoreType.DMA((NB,)),
        ],
        compiler_params=pltpu.CompilerParams(vmem_limit_bytes=52 << 20),
    )(values)
    scale = row_scale.reshape(NB, BS)
    pick = slot_picks(block_columns, live_slots)

    def apply(field, fine):
        return pl.pallas_call(
            lambda *refs: apply_kernel(fine, *refs),
            out_shape=FIELD,
            in_specs=[VMEM] * 6,
            out_specs=VMEM,
            compiler_params=PARAMS,
        )(pick, *exchange(field, rows, cols), values, scale)

    u1 = apply(u0, False)
    u2 = apply(u1, True)
    u3 = apply(u2, True)
    plane = lax.axis_size(PLANE)
    depth = lax.axis_size("z")
    parts = pl.pallas_call(
        last_kernel,
        out_shape=jax.ShapeDtypeStruct((plane, 1, BS), F32),
        in_specs=[VMEM] * 9,
        out_specs=VMEM,
        compiler_params=PARAMS,
    )(pick, *exchange(u3, rows, cols), values, scale, u0, u1, u2)
    parts = lax.all_to_all(parts, PLANE, split_axis=0, concat_axis=0, tiled=True)
    parts = pl.pallas_call(
        sum_kernel,
        out_shape=jax.ShapeDtypeStruct((depth, 1, BS), F32),
        in_specs=[VMEM],
        out_specs=VMEM,
        compiler_params=PARAMS,
    )(parts)
    parts = lax.all_to_all(parts, "z", split_axis=0, concat_axis=0, tiled=True)
    solution_field, hessenberg = pl.pallas_call(
        finish_kernel,
        out_shape=(FIELD, jax.ShapeDtypeStruct((ITERS, ITERS + 1), F32)),
        in_specs=[VMEM] * 5,
        out_specs=(VMEM, VMEM),
        compiler_params=PARAMS,
    )(parts, u0, u1, u2, u3)
    return solution_field.reshape(right_side.shape), hessenberg.T


def solution(mesh):
    rows, cols = mesh.shape["row"], mesh.shape["col"]
    finer = Mesh(
        mesh.devices.reshape(4, rows // 4, cols // 2, 2), ("y", "z", "x", "core")
    )
    in_specs = (
        P(ROW, COL, None, None),
        P(ROW, COL, None, None, None, None),
        P(ROW, COL, None, None),
        P(ROW, COL, None),
        P(ROW, COL, None, None),
    )
    out_specs = (P(ROW, COL, None, None), P())
    return jax.shard_map(
        lambda *arrays: on_device(rows, cols, *arrays),
        mesh=finer,
        in_specs=in_specs,
        out_specs=out_specs,
        check_vma=False,
    )
```
